32 devices in a mesh: fsdp: 4 (over z), ty: 4 (over y, core), tx: 2 (over x).
Axes of the slice: x: 2, y: 2, z: 4, core: 2. Of those that a mesh axis runs over, the one named last changes fastest.
Arguments:
- q_raw: bfloat16 [8, 32, 16, 1536], P('fsdp', 'ty', 'tx'), may hold values from -6 to 6
- k_raw: bfloat16 [8, 32, 16, 1536], P('fsdp', 'ty', 'tx'), may hold values from -6 to 6
- values: bfloat16 [8, 32, 16, 1536], P('fsdp', 'ty', 'tx'), may hold values from -6 to 6
- d_out: bfloat16 [8, 32, 16, 1536], P('fsdp', 'ty', 'tx'), may hold values from -6 to 6
- q_gain: float32 [128], P('fsdp'), may hold values from 0.1 to 1.9
- k_gain: float32 [128], P('fsdp'), may hold values from 0.1 to 1.9
- windows: int32 [12, 2], replicated, may hold values from 1 to 3, as said below
Outputs:
- out: bfloat16 [8, 32, 16, 1536], P('fsdp', 'ty', 'tx')
- q_grad: bfloat16 [8, 32, 16, 1536], P('fsdp', 'ty', 'tx')
- k_grad: bfloat16 [8, 32, 16, 1536], P('fsdp', 'ty', 'tx')
- v_grad: bfloat16 [8, 32, 16, 1536], P('fsdp', 'ty', 'tx')
- q_gain_grad: float32 [128], P('fsdp')
- k_gain_grad: float32 [128], P('fsdp')
The draws below stay inside these ranges and needn't reach their ends.
Inputs may be any that keep to these rules, and one draw needn't show every extreme that they name: `windows`: every entry is 1 or 3; in each of the two columns some head has 3.
All inputs are finite; a program needn't handle non-finite values.
Results may differ from the reference program's by a relative error of at most 0.0083.
Values may be sent and summed in bfloat16 or wider, within the bound.
A program may use at most 64 MiB of HBM per device.

```python
import math
import jax
import jax.numpy as jnp
from jax import lax

HEADS = 12
HEAD_DIM = 128
TILE = 8
FRAMES = 8
HEIGHT = 32
WIDTH = 16


def draw_windows(key, part):
    reach_base = jax.random.randint(jax.random.fold_in(key, 11), (HEADS, 2), 0, 2)
    chosen = jax.random.randint(jax.random.fold_in(key, 12), (2,), 0, HEADS)
    forced = (jnp.arange(HEADS)[:, None] == chosen[None, :]).astype(jnp.int32)
    return (2 * jnp.maximum(reach_base, forced) + 1).astype(jnp.int32)


def level_of(own_key, dims, cuts, smallest, largest):
    def one(dim, parts):
        draws = jax.random.uniform(jax.random.fold_in(jax.random.fold_in(own_key, 6), dim), (parts,), jnp.float32, smallest / len(cuts), largest / len(cuts))
        return jnp.repeat(jnp.exp(draws), dims[dim] // parts).reshape((-1,) + (1,) * (len(dims) - dim - 1))

    gain = one(*cuts[0])
    for cut in cuts[1:]:
        gain = gain * one(*cut)
    return gain


def noise(rng, shape, scale, reach, cuts=(), kind=jnp.bfloat16):
    values = scale * jax.random.normal(rng, shape, jnp.float32)
    if cuts:
        values = values * level_of(rng, shape, cuts, -0.22, 0.18)
    return jnp.clip(values, -reach, reach).astype(kind)


def setup_inputs(seed: int = 0) -> dict:
    key_of = jax.random.split(jax.random.key(seed), 8)
    q_raw = noise(key_of[0], (FRAMES, HEIGHT, WIDTH, HEADS * HEAD_DIM), 1.0, 6.0, ((0, 4), (1, 4), (2, 2)))
    k_raw = noise(key_of[1], (FRAMES, HEIGHT, WIDTH, HEADS * HEAD_DIM), 1.0, 6.0, ((0, 4), (1, 4), (2, 2)))
    values = noise(key_of[2], (FRAMES, HEIGHT, WIDTH, HEADS * HEAD_DIM), 1.0, 6.0, ((0, 4), (1, 4), (2, 2)))
    d_out = noise(key_of[3], (FRAMES, HEIGHT, WIDTH, HEADS * HEAD_DIM), 1.0, 6.0, ((0, 4), (1, 4), (2, 2)))
    q_gain = jnp.clip(1.0 + 0.18 * jax.random.normal(key_of[4], (HEAD_DIM,), jnp.float32), 0.1, 1.9)
    k_gain = jnp.clip(1.0 + 0.18 * jax.random.normal(key_of[5], (HEAD_DIM,), jnp.float32), 0.1, 1.9)
    windows = draw_windows(jax.random.fold_in(key_of[7], 71), 0)
    return {"q_raw": q_raw, "k_raw": k_raw, "values": values, "d_out": d_out, "q_gain": q_gain, "k_gain": k_gain, "windows": windows}


NORM_EPS = 1e-06
NEIGHBOUR_STEPS = [(row_step, col_step) for row_step in (-1, 0, 1) for col_step in (-1, 0, 1)]

def product(form, left, right):
    return jnp.einsum(form, left.astype(jnp.float32), right.astype(jnp.float32), precision=lax.Precision.HIGHEST)

def to_tiles(field_grid, tile_size):
    row_count, col_count, feature_count = field_grid.shape
    shaped = field_grid.reshape(row_count // tile_size, tile_size, col_count // tile_size, tile_size, feature_count)
    return shaped.transpose(0, 2, 1, 3, 4).reshape(row_count // tile_size, col_count // tile_size, tile_size * tile_size, feature_count)

def from_tiles(tile_view, tile_size):
    tile_rows, tile_cols, cell_count, feature_count = tile_view.shape
    shaped = tile_view.reshape(tile_rows, tile_cols, tile_size, tile_size, feature_count).transpose(0, 2, 1, 3, 4)
    return shaped.reshape(tile_rows * tile_size, tile_cols * tile_size, feature_count)

def neighbours(padded):
    tile_rows = padded.shape[0] - 2
    tile_cols = padded.shape[1] - 2
    shifted_views = [padded[1 + row_step:1 + row_step + tile_rows, 1 + col_step:1 + col_step + tile_cols] for row_step, col_step in NEIGHBOUR_STEPS]
    return jnp.stack(shifted_views, axis=2)

def window_live(first_row, first_col, tile_rows, tile_cols, total_rows, total_cols, windows):
    reach_rows = (windows[:, 0] - 1) // 2
    reach_cols = (windows[:, 1] - 1) // 2
    row_index = first_row + jnp.arange(tile_rows, dtype=jnp.int32)
    col_index = first_col + jnp.arange(tile_cols, dtype=jnp.int32)
    pieces = []
    for row_step, col_step in NEIGHBOUR_STEPS:
        inside_rows = ((row_index + row_step >= 0) & (row_index + row_step < total_rows))[:, None, None]
        inside_cols = ((col_index + col_step >= 0) & (col_index + col_step < total_cols))[None, :, None]
        within = ((abs(row_step) <= reach_rows) & (abs(col_step) <= reach_cols))[None, None, :]
        pieces.append(inside_rows & inside_cols & within)
    return jnp.stack(pieces, axis=-1)

def normalize(raw_field, norm_gain, head_count):
    floats = raw_field.astype(jnp.float32)
    floats = floats.reshape(floats.shape[:-1] + (head_count, norm_gain.shape[0]))
    inverse = lax.rsqrt(lax.optimization_barrier(jnp.mean(floats * floats, axis=-1, keepdims=True)) + NORM_EPS)
    normed = floats * inverse
    return (normed, inverse, (normed * norm_gain).astype(jnp.bfloat16))

def norm_backward(upstream, normed, inverse, norm_gain):
    gain_part = lax.optimization_barrier(jnp.sum(upstream * normed, axis=tuple(range(upstream.ndim - 1))))
    scaled = upstream * norm_gain
    raw_grad = inverse * (scaled - normed * lax.optimization_barrier(jnp.mean(scaled * normed, axis=-1, keepdims=True)))
    return (raw_grad, gain_part)

def query_side(queries, keys_near, values_near, grad_out, window_open, score_scale):
    scores = product('yxqhc,yxnkhc->yxhqnk', queries, keys_near) * score_scale
    open_mask = window_open[:, :, :, None, :, None]
    weights = jnp.where(open_mask, jnp.exp(scores), 0.0)
    totals = lax.optimization_barrier(jnp.sum(weights, axis=(4, 5)))
    shares = weights / totals[..., None, None]
    shares_low = shares.astype(jnp.bfloat16)
    output = product('yxhqnk,yxnkhc->yxqhc', shares_low, values_near).astype(jnp.bfloat16)
    output_back = lax.optimization_barrier(output).astype(jnp.float32)
    row_delta = lax.optimization_barrier(jnp.sum(grad_out.astype(jnp.float32) * output_back, axis=-1))
    share_grad = product('yxqhc,yxnkhc->yxhqnk', grad_out, values_near)
    score_grad = (shares * (share_grad - jnp.swapaxes(row_delta, 2, 3)[..., None, None])).astype(jnp.bfloat16)
    query_grad = product('yxhqnk,yxnkhc->yxqhc', score_grad, keys_near) * score_scale
    return (output, jnp.swapaxes(totals, 2, 3), row_delta, query_grad)

def key_side(keys, value_tiles, queries_near, grads_near, totals_near, delta_near, window_open, score_scale):
    scores = product('yxnqhc,yxkhc->yxhnqk', queries_near, keys) * score_scale
    open_mask = window_open[:, :, :, :, None, None]
    weights = jnp.where(open_mask, jnp.exp(scores), 0.0)
    divisor = jnp.where(open_mask, jnp.moveaxis(totals_near, 4, 2)[..., None], 1.0)
    shares = weights / divisor
    shares_low = shares.astype(jnp.bfloat16)
    value_grad = product('yxhnqk,yxnqhc->yxkhc', shares_low, grads_near)
    share_grad = product('yxnqhc,yxkhc->yxhnqk', grads_near, value_tiles)
    score_grad = (shares * (share_grad - jnp.moveaxis(delta_near, 4, 2)[..., None])).astype(jnp.bfloat16)
    key_grad = product('yxhnqk,yxnqhc->yxkhc', score_grad, queries_near) * score_scale
    return (key_grad, value_grad)

def tiled(field_grid, head_count):
    tile_view = to_tiles(field_grid, TILE)
    return tile_view.reshape(tile_view.shape[:3] + (head_count, -1))

def to_field(tile_view):
    flat_view = tile_view.reshape(tile_view.shape[:3] + (-1,))
    return from_tiles(flat_view, TILE)

def padded_near(tile_view):
    pad_widths = ((1, 1), (1, 1)) + ((0, 0),) * (tile_view.ndim - 2)
    return neighbours(jnp.pad(tile_view, pad_widths))

def one_video(q_raw, k_raw, values, d_out, q_gain, k_gain, windows):
    row_count, col_count, feature_count = q_raw.shape
    score_scale = 1.0 / math.sqrt(HEAD_DIM)
    q_normed, q_inverse, q_hat = normalize(q_raw, q_gain, HEADS)
    k_normed, k_inverse, k_hat = normalize(k_raw, k_gain, HEADS)
    queries = tiled(q_hat.reshape(row_count, col_count, feature_count), HEADS)
    keys = tiled(k_hat.reshape(row_count, col_count, feature_count), HEADS)
    value_tiles = tiled(values, HEADS)
    grad_tiles = tiled(d_out, HEADS)
    tile_rows = row_count // TILE
    tile_cols = col_count // TILE
    window_open = window_live(0, 0, tile_rows, tile_cols, tile_rows, tile_cols, windows)
    keys_near = padded_near(keys)
    values_near = padded_near(value_tiles)

    def query_row(row_items):
        lifted = [item[None] for item in row_items]
        results = query_side(lifted[0], lifted[1], lifted[2], lifted[3], lifted[4], score_scale)
        return tuple((result[0] for result in results))
    output, totals, row_delta, query_grad = lax.map(query_row, (queries, keys_near, values_near, grad_tiles, window_open))
    queries_near = padded_near(queries)
    grads_near = padded_near(grad_tiles)
    totals_near = padded_near(totals)
    delta_near = padded_near(row_delta)

    def key_row(row_items):
        lifted = [item[None] for item in row_items]
        results = key_side(lifted[0], lifted[1], lifted[2], lifted[3], lifted[4], lifted[5], lifted[6], score_scale)
        return tuple((result[0] for result in results))
    key_grad, value_grad = lax.map(key_row, (keys, value_tiles, queries_near, grads_near, totals_near, delta_near, window_open))
    q_upstream = to_field(query_grad).reshape(q_normed.shape)
    k_upstream = to_field(key_grad).reshape(k_normed.shape)
    q_field_grad, q_part = norm_backward(q_upstream, q_normed, q_inverse, q_gain)
    k_field_grad, k_part = norm_backward(k_upstream, k_normed, k_inverse, k_gain)
    return (to_field(output), q_field_grad.reshape(row_count, col_count, feature_count).astype(jnp.bfloat16), k_field_grad.reshape(row_count, col_count, feature_count).astype(jnp.bfloat16), to_field(value_grad).astype(jnp.bfloat16), q_part, k_part)

def reference(q_raw, k_raw, values, d_out, q_gain, k_gain, windows):

    def video_step(video_items):
        return one_video(video_items[0], video_items[1], video_items[2], video_items[3], q_gain, k_gain, windows)
    output, q_grad, k_grad, v_grad, q_part, k_part = lax.map(video_step, (q_raw, k_raw, values, d_out))
    return (output, q_grad, k_grad, v_grad, lax.optimization_barrier(jnp.sum(q_part, axis=0)), lax.optimization_barrier(jnp.sum(k_part, axis=0)))
```

```python
import functools
import math

import jax
import jax.numpy as jnp
from jax import lax
from jax.experimental import pallas as pl
from jax.experimental.pallas import tpu as pltpu
from jax.sharding import PartitionSpec as P

TILE = 8
NORM_EPS = 1e-06
CLOSED = -1e30
MESH = pl.DeviceIdType.MESH
V, K, D, Q = 0, 1, 2, 3
UNROLL = 2


def dot_nt(left, right):
    return lax.dot_general(
        left, right, (((1,), (1,)), ((), ())), preferred_element_type=jnp.float32
    )


def dot_nn(left, right):
    return lax.dot_general(
        left, right, (((1,), (0,)), ((), ())), preferred_element_type=jnp.float32
    )


def norm_parts(raw):
    floats = raw.astype(jnp.float32)
    inverse = lax.rsqrt(jnp.mean(floats * floats, axis=-1, keepdims=True) + NORM_EPS)
    return floats * inverse, inverse


def when(cond, act):
    if cond is None:
        act()
    else:
        pl.when(cond)(act)


def both(one, two):
    if one is None:
        return two
    if two is None:
        return one
    return jnp.logical_and(one, two)


def kernel(
    dims,
    win_ref,
    gain_ref,
    q_ref,
    k_ref,
    v_ref,
    d_ref,
    out_ref,
    qg_ref,
    kg_ref,
    vg_ref,
    part_ref,
    near,
    stat,
    srow,
    bias,
    gains,
    gain_send,
    gain_recv,
    x_send,
    x_recv,
    ty_send,
    ty_recv,
):
    fsdp, ty, tx, frames, rows, heads, size, slots = dims
    width = heads * size
    z = lax.axis_index("fsdp")
    t = lax.axis_index("ty")
    x = lax.axis_index("tx")
    scale = 1.0 / math.sqrt(size)
    exp_scale = scale * math.log2(math.e)

    if tx == 1:
        x_links = []
    elif tx == 2:
        x_links = [(1, 1 - x, None, None)]
    else:
        x_links = [(1, x + 1, x < tx - 1, x > 0), (2, x - 1, x > 0, x < tx - 1)]
    ty_links = [(1, t + 1, t < ty - 1, t > 0), (2, t - 1, t > 0, t < ty - 1)]

    barrier = pltpu.get_barrier_semaphore()

    def greet(cond, device):
        when(cond, lambda: pl.semaphore_signal(
            barrier, inc=1, device_id=device, device_id_type=MESH))

    for step in range(1, fsdp):
        greet(None, {"fsdp": lax.rem(z + step, fsdp)})
    for _, peer, sends, _ in x_links:
        greet(sends, {"tx": peer})
    for _, peer, sends, _ in ty_links:
        greet(sends, {"ty": peer})

    def block(buffer, chunk, slot):
        if buffer is stat:
            return stat.at[chunk, slot]
        array, frame = chunk
        return near.at[array, frame, pl.ds(slot * rows, rows)]

    def sem_index(buffer, chunk):
        if buffer is stat:
            return 4 * frames + chunk
        return chunk[0] * frames + chunk[1]

    def x_copy(link, buffer, chunk):
        column, peer, _, _ = link
        s = sem_index(buffer, chunk)
        return pltpu.make_async_remote_copy(
            src_ref=block(buffer, chunk, 0),
            dst_ref=block(buffer, chunk, 3 * column),
            send_sem=x_send.at[column - 1, s],
            recv_sem=x_recv.at[column - 1, s],
            device_id={"tx": peer},
            device_id_type=MESH,
        )

    def ty_copy(link, column, buffer, chunk):
        row, peer, _, _ = link
        s = sem_index(buffer, chunk)
        return pltpu.make_async_remote_copy(
            src_ref=block(buffer, chunk, 3 * column),
            dst_ref=block(buffer, chunk, 3 * column + row),
            send_sem=ty_send.at[row - 1, column, s],
            recv_sem=ty_recv.at[row - 1, column, s],
            device_id={"ty": peer},
            device_id_type=MESH,
        )

    def start_x(buffer, chunk):
        for link in x_links:
            when(link[2], lambda link=link: x_copy(link, buffer, chunk).start())

    def start_ty(buffer, chunk):
        for link in ty_links:
            when(link[2], lambda link=link: ty_copy(link, 0, buffer, chunk).start())

    def forward(buffer, chunk):
        for x_link in x_links:
            when(x_link[3], lambda x_link=x_link: x_copy(x_link, buffer, chunk).wait_recv())
            for link in ty_links:
                when(
                    both(link[2], x_link[3]),
                    lambda link=link, x_link=x_link: ty_copy(
                        link, x_link[0], buffer, chunk).start(),
                )

    def arrive(buffer, chunk):
        for link in ty_links:
            when(link[3], lambda link=link: ty_copy(link, 0, buffer, chunk).wait_recv())
            for x_link in x_links:
                when(
                    both(link[3], x_link[3]),
                    lambda link=link, x_link=x_link: ty_copy(
                        link, x_link[0], buffer, chunk).wait_recv(),
                )

    def finish(buffer, chunk):
        for link in x_links:
            when(link[2], lambda link=link: x_copy(link, buffer, chunk).wait_send())
        for link in ty_links:
            when(link[2], lambda link=link: ty_copy(link, 0, buffer, chunk).wait_send())
            for x_link in x_links:
                when(
                    both(link[2], x_link[3]),
                    lambda link=link, x_link=x_link: ty_copy(
                        link, x_link[0], buffer, chunk).wait_send(),
                )

    def clear(slot):
        near[:, :, slot * rows:(slot + 1) * rows, :] = jnp.zeros(
            (4, frames, rows, width), near.dtype)
        stat[:, slot] = jnp.zeros((frames,) + stat.shape[2:], stat.dtype)

    exists = [None] * slots
    for column in range(slots // 3):
        have_column = None
        for link in x_links:
            if link[0] == column:
                have_column = link[3]
        exists[3 * column] = have_column
        for link in ty_links:
            exists[3 * column + link[0]] = both(link[3], have_column)
    for slot in range(slots):
        if slot >= 3 * (slots // 3):
            exists[slot] = False
            clear(slot)
        elif exists[slot] is not None:
            pl.when(jnp.logical_not(exists[slot]))(functools.partial(clear, slot))

    lane = lax.broadcasted_iota(jnp.int32, (1, 2 * rows), 1)
    for head in range(heads):
        row_bias = jnp.where(win_ref[head, 0] >= 3, 0.0, CLOSED)
        col_bias = jnp.where(win_ref[head, 1] >= 3, 0.0, CLOSED)
        terms = []
        for slot in range(slots):
            term = jnp.float32(0.0)
            if slot % 3 != 0:
                term = term + row_bias
            if slot // 3 != 0:
                term = term + col_bias
            if exists[slot] is False:
                term = jnp.float32(CLOSED)
            elif exists[slot] is not None:
                term = term + jnp.where(exists[slot], 0.0, CLOSED)
            terms.append(term)
        for pair in range(slots // 2):
            bias[head:head + 1, pair * 2 * rows:(pair + 1) * 2 * rows] = jnp.where(
                lane < rows, terms[2 * pair], terms[2 * pair + 1])

    for frame in range(frames):
        span = slice(frame * rows, (frame + 1) * rows)
        near[V, frame, 0:rows, :] = v_ref[span, :]
        near[D, frame, 0:rows, :] = d_ref[span, :]
    gains[pl.ds(z, 1)] = gain_ref[...][None]

    greeted = fsdp - 1
    for _, _, _, receives in x_links + ty_links:
        greeted = greeted + (1 if receives is None else receives.astype(jnp.int32))
    pl.semaphore_wait(barrier, greeted)

    def gain_copy(step):
        return pltpu.make_async_remote_copy(
            src_ref=gain_ref,
            dst_ref=gains.at[z],
            send_sem=gain_send.at[step - 1],
            recv_sem=gain_recv.at[step - 1],
            device_id={"fsdp": lax.rem(z + step, fsdp)},
            device_id_type=MESH,
        )

    for step in range(1, fsdp):
        gain_copy(step).start()
    start_x(near, (V, 0))
    start_ty(near, (V, 0))
    for step in range(1, fsdp):
        gain_copy(step).wait()
    gain_all = jnp.sum(gains[...], axis=0)
    q_gain = gain_all[0:1]
    k_gain = gain_all[1:2]

    def place(source, array, frame, gain):
        def one(head, carry):
            cols = pl.ds(pl.multiple_of(head * size, size), size)
            normed, _ = norm_parts(source[frame * rows:(frame + 1) * rows, cols])
            near[array, frame, 0:rows, cols] = (normed * gain).astype(near.dtype)
            return carry

        lax.fori_loop(0, heads, one, 0)

    place(k_ref, K, 0, k_gain)
    start_x(near, (K, 0))
    start_ty(near, (K, 0))
    for frame in range(1, frames):
        start_x(near, (V, frame))
        place(k_ref, K, frame, k_gain)
        start_x(near, (K, frame))
    for frame in range(frames):
        start_x(near, (D, frame))
        place(q_ref, Q, frame, q_gain)
        start_x(near, (Q, frame))

    stat_lane = lax.broadcasted_iota(jnp.int32, (rows, stat.shape[3]), 1)

    def backward(raw, upstream, gain):
        normed, inverse = norm_parts(raw)
        part = jnp.sum(upstream * normed, axis=0, keepdims=True)
        scaled = upstream * gain
        mean = jnp.mean(scaled * normed, axis=-1, keepdims=True)
        return inverse * (scaled - normed * mean), part

    def query_head(frame, head, held, part):
        cols = pl.ds(pl.multiple_of(head * size, size), size)
        span = slice(frame * rows, (frame + 1) * rows)
        keys = near[K, frame, :, cols]
        vals = near[V, frame, :, cols]
        queries = near[Q, frame, 0:rows, cols]
        grads = near[D, frame, 0:rows, cols]
        weights = jnp.exp2(dot_nt(queries, keys) * exp_scale + bias[pl.ds(head, 1), :])
        inverse = 1.0 / jnp.sum(weights, axis=-1, keepdims=True)
        shares = weights * inverse
        output = dot_nn(shares.astype(jnp.bfloat16), vals).astype(jnp.bfloat16)
        out_ref[span, cols] = output
        delta = jnp.sum(
            grads.astype(jnp.float32) * output.astype(jnp.float32), axis=-1, keepdims=True)
        share_grad = dot_nt(grads, vals)
        score_grad = (shares * (share_grad - delta)).astype(jnp.bfloat16)
        raw_grad, more = backward(
            q_ref[span, cols], dot_nn(score_grad, keys) * scale, q_gain)
        qg_ref[span, cols] = raw_grad.astype(jnp.bfloat16)
        held = jnp.where(stat_lane == head, inverse, held)
        held = jnp.where(stat_lane == 16 + head, delta, held)
        return held, part + more

    def query_side(frame, part):
        def some(step, carry):
            held, part = carry
            for k in range(UNROLL):
                held, part = query_head(frame, step * UNROLL + k, held, part)
            return held, part

        held, part = lax.fori_loop(
            0, heads // UNROLL, some,
            (jnp.zeros((rows, stat.shape[3]), jnp.float32), part))
        turned = jnp.transpose(jnp.concatenate([held, held], axis=0))
        stat[frame, 0] = turned[0:stat.shape[2]]
        return part

    def key_head(frame, head, part):
        cols = pl.ds(pl.multiple_of(head * size, size), size)
        span = slice(frame * rows, (frame + 1) * rows)
        keys = near[K, frame, 0:rows, cols]
        vals = near[V, frame, 0:rows, cols]
        queries = near[Q, frame, :, cols]
        grads = near[D, frame, :, cols]
        weights = jnp.exp2(dot_nt(keys, queries) * exp_scale + bias[pl.ds(head, 1), :])
        shares = weights * srow[pl.ds(head, 1), :]
        vg_ref[span, cols] = dot_nn(shares.astype(jnp.bfloat16), grads).astype(jnp.bfloat16)
        share_grad = dot_nt(vals, grads)
        score_grad = (shares * (share_grad - srow[pl.ds(16 + head, 1), :])).astype(jnp.bfloat16)
        raw_grad, more = backward(
            k_ref[span, cols], dot_nn(score_grad, queries) * scale, k_gain)
        kg_ref[span, cols] = raw_grad.astype(jnp.bfloat16)
        return part + more

    def key_side(frame, part):
        side = lax.broadcasted_iota(jnp.int32, (stat.shape[2], 2 * rows), 1)
        for pair in range(slots // 2):
            srow[:, pair * 2 * rows:(pair + 1) * 2 * rows] = jnp.where(
                side < rows, stat[frame, 2 * pair], stat[frame, 2 * pair + 1])

        def some(step, part):
            for k in range(UNROLL):
                part = key_head(frame, step * UNROLL + k, part)
            return part

        return lax.fori_loop(0, heads // UNROLL, some, part)

    pairs = [(V, K, frame) for frame in range(frames)]
    pairs += [(D, Q, frame) for frame in range(frames)]
    part = jnp.zeros((1, size), jnp.float32)
    for place_in, (first, second, frame) in enumerate(pairs):
        forward(near, (first, frame))
        forward(near, (second, frame))
        if place_in + 1 < len(pairs):
            later = pairs[place_in + 1]
            start_ty(near, (later[0], later[2]))
            start_ty(near, (later[1], later[2]))
        if first == D:
            forward(stat, frame)
        arrive(near, (first, frame))
        arrive(near, (second, frame))
        if first == V:
            part = query_side(frame, part)
            start_x(stat, frame)
            start_ty(stat, frame)
            if frame == frames - 1:
                part_ref[0:1, :] = part
                part = jnp.zeros((1, size), jnp.float32)
        else:
            arrive(stat, frame)
            part = key_side(frame, part)
    part_ref[1:2, :] = part
    part_ref[2:8, :] = jnp.zeros((6, size), jnp.float32)

    for frame in range(frames):
        for array in range(4):
            finish(near, (array, frame))
        finish(stat, frame)


def body(axes, q_raw, k_raw, values, d_out, q_gain, k_gain, windows):
    fsdp, ty, tx = axes
    frames, height, across, width = q_raw.shape
    rows = height * across
    heads = windows.shape[0]
    size = width // heads
    columns = min(tx, 3)
    slots = 3 * columns + (3 * columns) % 2
    share = q_gain.shape[0]
    mine = jnp.arange(size, dtype=jnp.int32) // share == lax.axis_index("fsdp")
    placed = jnp.where(
        mine[None, :], jnp.stack([jnp.tile(q_gain, fsdp), jnp.tile(k_gain, fsdp)]), 0.0)
    placed = jnp.pad(placed, ((0, 6), (0, 0)))

    flat = (frames * rows, width)
    field = jax.ShapeDtypeStruct(flat, jnp.bfloat16)
    vmem = pl.BlockSpec(memory_space=pltpu.VMEM)
    sems = 5 * frames
    dims = (fsdp, ty, tx, frames, rows, heads, size, slots)
    dma = pltpu.SemaphoreType.DMA
    side = max(columns - 1, 1)
    output, q_grad, k_grad, v_grad, parts = pl.pallas_call(
        functools.partial(kernel, dims),
        out_shape=[field] * 4 + [jax.ShapeDtypeStruct((8, size), jnp.float32)],
        in_specs=[pl.BlockSpec(memory_space=pltpu.SMEM)] + [vmem] * 5,
        out_specs=[vmem] * 5,
        scratch_shapes=[
            pltpu.VMEM((4, frames, slots * rows, width), jnp.bfloat16),
            pltpu.VMEM((frames, slots, 32, 2 * rows), jnp.float32),
            pltpu.VMEM((32, slots * rows), jnp.float32),
            pltpu.VMEM((16, slots * rows), jnp.float32),
            pltpu.VMEM((fsdp, 8, size), jnp.float32),
            dma((max(fsdp - 1, 1),)),
            dma((max(fsdp - 1, 1),)),
            dma((side, sems)),
            dma((side, sems)),
            dma((2, columns, sems)),
            dma((2, columns, sems)),
        ],
        compiler_params=pltpu.CompilerParams(
            collective_id=0, has_side_effects=True, vmem_limit_bytes=48 * 1024 * 1024),
    )(
        windows,
        placed,
        q_raw.reshape(flat),
        k_raw.reshape(flat),
        values.reshape(flat),
        d_out.reshape(flat),
    )
    whole_sum = lax.psum(parts[0:2], ("fsdp", "ty", "tx"))
    owned = lax.dynamic_slice_in_dim(whole_sum, lax.axis_index("fsdp") * share, share, 1)
    return (
        output.reshape(q_raw.shape),
        q_grad.reshape(q_raw.shape),
        k_grad.reshape(q_raw.shape),
        v_grad.reshape(q_raw.shape),
        owned[0],
        owned[1],
    )


def solution(mesh):
    axes = tuple(mesh.shape[name] for name in ("fsdp", "ty", "tx"))
    spec = P("fsdp", "ty", "tx", None)
    return jax.shard_map(
        functools.partial(body, axes),
        mesh=mesh,
        in_specs=(spec, spec, spec, spec, P("fsdp"), P("fsdp"), P()),
        out_specs=(spec, spec, spec, spec, P("fsdp"), P("fsdp")),
        check_vma=False,
    )
```

```python
import functools
import math

import jax
import jax.numpy as jnp
from jax import lax
from jax.experimental import pallas as pl
from jax.experimental.pallas import tpu as pltpu
from jax.sharding import PartitionSpec as P

TILE = 8
NORM_EPS = 1e-06
CLOSED = -1e30
MESH = pl.DeviceIdType.MESH
V, K, D, Q = 0, 1, 2, 3
UNROLL = 4


def dot_nt(left, right):
    return lax.dot_general(
        left, right, (((1,), (1,)), ((), ())), preferred_element_type=jnp.float32
    )


def dot_nn(left, right):
    return lax.dot_general(
        left, right, (((1,), (0,)), ((), ())), preferred_element_type=jnp.float32
    )


def norm_parts(raw):
    floats = raw.astype(jnp.float32)
    inverse = lax.rsqrt(jnp.mean(floats * floats, axis=-1, keepdims=True) + NORM_EPS)
    return floats * inverse, inverse


def when(cond, act):
    if cond is None:
        act()
    else:
        pl.when(cond)(act)


def both(one, two):
    if one is None:
        return two
    if two is None:
        return one
    return jnp.logical_and(one, two)


def kernel(
    dims,
    win_ref,
    q_gain_ref,
    k_gain_ref,
    q_hbm,
    k_hbm,
    v_hbm,
    d_hbm,
    out_ref,
    qg_ref,
    kg_ref,
    vg_ref,
    q_part_ref,
    k_part_ref,
    near,
    stat,
    srow,
    bias,
    gains,
    q_ref,
    k_ref,
    sums,
    load_sem,
    gain_send,
    gain_recv,
    sum_send,
    sum_recv,
    x_send,
    x_recv,
    ty_send,
    ty_recv,
):
    fsdp, ty, tx, frames, rows, heads, size, slots = dims
    width = heads * size
    z = lax.axis_index("fsdp")
    t = lax.axis_index("ty")
    x = lax.axis_index("tx")
    scale = 1.0 / math.sqrt(size)
    exp_scale = scale * math.log2(math.e)

    if tx == 1:
        x_links = []
    elif tx == 2:
        x_links = [(1, 1 - x, None, None)]
    else:
        x_links = [(1, x + 1, x < tx - 1, x > 0), (2, x - 1, x > 0, x < tx - 1)]
    ty_links = [(1, t + 1, t < ty - 1, t > 0), (2, t - 1, t > 0, t < ty - 1)]

    barrier = pltpu.get_barrier_semaphore()

    def greet(device):
        pl.semaphore_signal(barrier, inc=1, device_id=device, device_id_type=MESH)

    lines = (("fsdp", z, fsdp), ("tx", x, tx), ("ty", t, ty))
    for axis, place_in, count in lines:
        for step in range(1, count):
            greet({axis: lax.rem(place_in + step, count)})

    loads = [
        pltpu.make_async_copy(source.at[frame * rows:(frame + 1) * rows], target, load_sem.at[i])
        for i, (source, frame, target) in enumerate(
            [(v_hbm, frame, near.at[V, frame, 0:rows]) for frame in range(frames)]
            + [(k_hbm, frame, k_ref.at[frame * rows:(frame + 1) * rows]) for frame in range(frames)]
            + [(d_hbm, frame, near.at[D, frame, 0:rows]) for frame in range(frames)]
            + [(q_hbm, frame, q_ref.at[frame * rows:(frame + 1) * rows]) for frame in range(frames)])
    ]
    for load in loads:
        load.start()

    def block(buffer, chunk, slot):
        if buffer is stat:
            return stat.at[chunk, slot]
        array, frame = chunk
        return near.at[array, frame, pl.ds(slot * rows, rows)]

    def sem_index(buffer, chunk):
        if buffer is stat:
            return 4 * frames + chunk
        return chunk[0] * frames + chunk[1]

    def x_copy(link, buffer, chunk):
        column, peer, _, _ = link
        s = sem_index(buffer, chunk)
        return pltpu.make_async_remote_copy(
            src_ref=block(buffer, chunk, 0),
            dst_ref=block(buffer, chunk, 3 * column),
            send_sem=x_send.at[column - 1, s],
            recv_sem=x_recv.at[column - 1, s],
            device_id={"tx": peer},
            device_id_type=MESH,
        )

    def ty_copy(link, column, buffer, chunk):
        row, peer, _, _ = link
        s = sem_index(buffer, chunk)
        return pltpu.make_async_remote_copy(
            src_ref=block(buffer, chunk, 3 * column),
            dst_ref=block(buffer, chunk, 3 * column + row),
            send_sem=ty_send.at[row - 1, column, s],
            recv_sem=ty_recv.at[row - 1, column, s],
            device_id={"ty": peer},
            device_id_type=MESH,
        )

    def start_x(buffer, chunk):
        for link in x_links:
            when(link[2], lambda link=link: x_copy(link, buffer, chunk).start())

    def start_ty(buffer, chunk):
        for link in ty_links:
            when(link[2], lambda link=link: ty_copy(link, 0, buffer, chunk).start())

    def forward(buffer, chunk):
        for x_link in x_links:
            when(x_link[3], lambda x_link=x_link: x_copy(x_link, buffer, chunk).wait_recv())
            for link in ty_links:
                when(
                    both(link[2], x_link[3]),
                    lambda link=link, x_link=x_link: ty_copy(
                        link, x_link[0], buffer, chunk).start(),
                )

    def arrive(buffer, chunk):
        for link in ty_links:
            when(link[3], lambda link=link: ty_copy(link, 0, buffer, chunk).wait_recv())
            for x_link in x_links:
                when(
                    both(link[3], x_link[3]),
                    lambda link=link, x_link=x_link: ty_copy(
                        link, x_link[0], buffer, chunk).wait_recv(),
                )

    def finish(buffer, chunk):
        for link in x_links:
            when(link[2], lambda link=link: x_copy(link, buffer, chunk).wait_send())
        for link in ty_links:
            when(link[2], lambda link=link: ty_copy(link, 0, buffer, chunk).wait_send())
            for x_link in x_links:
                when(
                    both(link[2], x_link[3]),
                    lambda link=link, x_link=x_link: ty_copy(
                        link, x_link[0], buffer, chunk).wait_send(),
                )

    def clear(slot):
        near[:, :, slot * rows:(slot + 1) * rows, :] = jnp.zeros(
            (4, frames, rows, width), near.dtype)
        stat[:, slot] = jnp.zeros((frames,) + stat.shape[2:], stat.dtype)

    exists = [None] * slots
    for column in range(slots // 3):
        have_column = None
        for link in x_links:
            if link[0] == column:
                have_column = link[3]
        exists[3 * column] = have_column
        for link in ty_links:
            exists[3 * column + link[0]] = both(link[3], have_column)
    for slot in range(slots):
        if slot >= 3 * (slots // 3):
            exists[slot] = False
            clear(slot)
        elif exists[slot] is not None:
            pl.when(jnp.logical_not(exists[slot]))(functools.partial(clear, slot))

    lane = lax.broadcasted_iota(jnp.int32, (1, 2 * rows), 1)
    for head in range(heads):
        row_bias = jnp.where(win_ref[0, head] >= 3, 0.0, CLOSED)
        col_bias = jnp.where(win_ref[1, head] >= 3, 0.0, CLOSED)
        terms = []
        for slot in range(slots):
            term = jnp.float32(0.0)
            if slot % 3 != 0:
                term = term + row_bias
            if slot // 3 != 0:
                term = term + col_bias
            if exists[slot] is False:
                term = jnp.float32(CLOSED)
            elif exists[slot] is not None:
                term = term + jnp.where(exists[slot], 0.0, CLOSED)
            terms.append(term)
        for pair in range(slots // 2):
            bias[head:head + 1, pair * 2 * rows:(pair + 1) * 2 * rows] = jnp.where(
                lane < rows, terms[2 * pair], terms[2 * pair + 1])

    share = size // fsdp
    gains[z] = jnp.zeros((8, size), jnp.float32)
    gains[z, 0:1, 0:share] = q_gain_ref[...]
    gains[z, 1:2, 0:share] = k_gain_ref[...]
    gains[z] = pltpu.roll(gains[z], z * share, 1)

    pl.semaphore_wait(barrier, fsdp + tx + ty - 3)

    def gain_copy(step):
        return pltpu.make_async_remote_copy(
            src_ref=gains.at[z],
            dst_ref=gains.at[z],
            send_sem=gain_send.at[step - 1],
            recv_sem=gain_recv.at[step - 1],
            device_id={"fsdp": lax.rem(z + step, fsdp)},
            device_id_type=MESH,
        )

    for step in range(1, fsdp):
        gain_copy(step).start()
    loads[0].wait()
    start_x(near, (V, 0))
    start_ty(near, (V, 0))
    for load in loads[1:]:
        load.wait()
    for step in range(1, fsdp):
        gain_copy(step).wait()
    gain_all = jnp.sum(gains[...], axis=0)
    q_gain = gain_all[0:1]
    k_gain = gain_all[1:2]

    def place(source, array, frame, gain):
        def one(head, carry):
            cols = pl.ds(pl.multiple_of(head * size, size), size)
            normed, _ = norm_parts(source[frame * rows:(frame + 1) * rows, cols])
            near[array, frame, 0:rows, cols] = (normed * gain).astype(near.dtype)
            return carry

        lax.fori_loop(0, heads, one, 0)

    place(k_ref, K, 0, k_gain)
    start_x(near, (K, 0))
    start_ty(near, (K, 0))
    for frame in range(1, frames):
        start_x(near, (V, frame))
        place(k_ref, K, frame, k_gain)
        start_x(near, (K, frame))
    for frame in range(frames):
        start_x(near, (D, frame))
        place(q_ref, Q, frame, q_gain)
        start_x(near, (Q, frame))

    stat_lane = lax.broadcasted_iota(jnp.int32, (rows, stat.shape[3]), 1)

    def backward(raw, upstream, gain):
        normed, inverse = norm_parts(raw)
        part = jnp.sum(upstream * normed, axis=0, keepdims=True)
        scaled = upstream * gain
        mean = jnp.mean(scaled * normed, axis=-1, keepdims=True)
        return inverse * (scaled - normed * mean), part

    def query_head(frame, head, held, part):
        cols = pl.ds(pl.multiple_of(head * size, size), size)
        span = slice(frame * rows, (frame + 1) * rows)
        keys = near[K, frame, :, cols]
        vals = near[V, frame, :, cols]
        queries = near[Q, frame, 0:rows, cols]
        grads = near[D, frame, 0:rows, cols]
        weights = jnp.exp2(dot_nt(queries, keys) * exp_scale + bias[pl.ds(head, 1), :])
        inverse = 1.0 / jnp.sum(weights, axis=-1, keepdims=True)
        shares = weights * inverse
        output = dot_nn(shares.astype(jnp.bfloat16), vals).astype(jnp.bfloat16)
        out_ref[span, cols] = output
        delta = jnp.sum(
            grads.astype(jnp.float32) * output.astype(jnp.float32), axis=-1, keepdims=True)
        share_grad = dot_nt(grads, vals)
        score_grad = (shares * (share_grad - delta)).astype(jnp.bfloat16)
        raw_grad, more = backward(
            q_ref[span, cols], dot_nn(score_grad, keys) * scale, q_gain)
        qg_ref[span, cols] = raw_grad.astype(jnp.bfloat16)
        held = jnp.where(stat_lane == head, inverse, held)
        held = jnp.where(stat_lane == 16 + head, delta, held)
        return held, part + more

    def query_side(frame, part):
        def some(step, carry):
            held, part = carry
            for k in range(UNROLL):
                held, part = query_head(frame, step * UNROLL + k, held, part)
            return held, part

        held, part = lax.fori_loop(
            0, heads // UNROLL, some,
            (jnp.zeros((rows, stat.shape[3]), jnp.float32), part))
        turned = jnp.transpose(jnp.concatenate([held, held], axis=0))
        stat[frame, 0] = turned[0:stat.shape[2]]
        return part

    def key_head(frame, head, part):
        cols = pl.ds(pl.multiple_of(head * size, size), size)
        span = slice(frame * rows, (frame + 1) * rows)
        keys = near[K, frame, 0:rows, cols]
        vals = near[V, frame, 0:rows, cols]
        queries = near[Q, frame, :, cols]
        grads = near[D, frame, :, cols]
        weights = jnp.exp2(dot_nt(keys, queries) * exp_scale + bias[pl.ds(head, 1), :])
        shares = weights * srow[pl.ds(head, 1), :]
        vg_ref[span, cols] = dot_nn(shares.astype(jnp.bfloat16), grads).astype(jnp.bfloat16)
        share_grad = dot_nt(vals, grads)
        score_grad = (shares * (share_grad - srow[pl.ds(16 + head, 1), :])).astype(jnp.bfloat16)
        raw_grad, more = backward(
            k_ref[span, cols], dot_nn(score_grad, queries) * scale, k_gain)
        kg_ref[span, cols] = raw_grad.astype(jnp.bfloat16)
        return part + more

    def key_side(frame, part):
        side = lax.broadcasted_iota(jnp.int32, (stat.shape[2], 2 * rows), 1)
        for pair in range(slots // 2):
            srow[:, pair * 2 * rows:(pair + 1) * 2 * rows] = jnp.where(
                side < rows, stat[frame, 2 * pair], stat[frame, 2 * pair + 1])

        def some(step, part):
            for k in range(UNROLL):
                part = key_head(frame, step * UNROLL + k, part)
            return part

        return lax.fori_loop(0, heads // UNROLL, some, part)

    pairs = [(V, K, frame) for frame in range(frames)]
    pairs += [(D, Q, frame) for frame in range(frames)]
    part = jnp.zeros((1, size), jnp.float32)
    for place_in, (first, second, frame) in enumerate(pairs):
        forward(near, (first, frame))
        forward(near, (second, frame))
        if place_in + 1 < len(pairs):
            later = pairs[place_in + 1]
            start_ty(near, (later[0], later[2]))
            start_ty(near, (later[1], later[2]))
        if first == D:
            forward(stat, frame)
        arrive(near, (first, frame))
        arrive(near, (second, frame))
        if first == V:
            part = query_side(frame, part)
            start_x(stat, frame)
            start_ty(stat, frame)
            if frame == frames - 1:
                q_part = part
                part = jnp.zeros((1, size), jnp.float32)
        else:
            arrive(stat, frame)
            part = key_side(frame, part)
    side = lax.broadcasted_iota(jnp.int32, (8, size), 0)
    total = jnp.where(side == 0, q_part, jnp.where(side == 1, part, 0.0))
    first = 0
    for axis, place_in, count in lines:
        if count > 1:
            sums[first + place_in] = total

            def sum_copy(step, axis=axis, place_in=place_in, count=count, first=first):
                return pltpu.make_async_remote_copy(
                    src_ref=sums.at[first + place_in],
                    dst_ref=sums.at[first + place_in],
                    send_sem=sum_send.at[first + step],
                    recv_sem=sum_recv.at[first + step],
                    device_id={axis: lax.rem(place_in + step, count)},
                    device_id_type=MESH,
                )

            for step in range(1, count):
                sum_copy(step).start()
            for step in range(1, count):
                sum_copy(step).wait()
            total = jnp.sum(sums[first:first + count], axis=0)
        first += count
    owned = pltpu.roll(total, lax.rem(size - z * share, size), 1)
    q_part_ref[...] = owned[0:1, 0:share]
    k_part_ref[...] = owned[1:2, 0:share]

    for frame in range(frames):
        for array in range(4):
            finish(near, (array, frame))
        finish(stat, frame)


def store(*refs):
    copies = [
        pltpu.make_async_copy(refs[i], refs[4 + i], refs[8].at[i]) for i in range(4)
    ]
    for copy in copies:
        copy.start()
    for copy in copies:
        copy.wait()


def body(axes, q_raw, k_raw, values, d_out, q_gain, k_gain, windows):
    fsdp, ty, tx = axes
    frames, height, across, width = q_raw.shape
    rows = height * across
    heads = windows.shape[0]
    size = width // heads
    columns = min(tx, 3)
    slots = 3 * columns + (3 * columns) % 2
    share = q_gain.shape[0]
    flat = (frames * rows, width)
    field = jax.ShapeDtypeStruct(flat, jnp.bfloat16)
    vmem = pl.BlockSpec(memory_space=pltpu.VMEM)
    sems = 5 * frames
    dims = (fsdp, ty, tx, frames, rows, heads, size, slots)
    dma = pltpu.SemaphoreType.DMA
    side = max(columns - 1, 1)
    hbm = pl.BlockSpec(memory_space=pltpu.HBM)
    gain_field = jax.ShapeDtypeStruct((1, share), jnp.float32)
    peers = fsdp + ty + tx
    *fields, q_part, k_part = pl.pallas_call(
        functools.partial(kernel, dims),
        out_shape=[field] * 4 + [gain_field] * 2,
        in_specs=[pl.BlockSpec(memory_space=pltpu.SMEM)] + [vmem] * 2 + [hbm] * 4,
        out_specs=[vmem] * 6,
        scratch_shapes=[
            pltpu.VMEM((4, frames, slots * rows, width), jnp.bfloat16),
            pltpu.VMEM((frames, slots, 32, 2 * rows), jnp.float32),
            pltpu.VMEM((32, slots * rows), jnp.float32),
            pltpu.VMEM((16, slots * rows), jnp.float32),
            pltpu.VMEM((fsdp, 8, size), jnp.float32),
            pltpu.VMEM(flat, jnp.bfloat16),
            pltpu.VMEM(flat, jnp.bfloat16),
            pltpu.VMEM((peers, 8, size), jnp.float32),
            dma((4 * frames,)),
            dma((max(fsdp - 1, 1),)),
            dma((max(fsdp - 1, 1),)),
            dma((peers,)),
            dma((peers,)),
            dma((side, sems)),
            dma((side, sems)),
            dma((2, columns, sems)),
            dma((2, columns, sems)),
        ],
        compiler_params=pltpu.CompilerParams(
            collective_id=0, has_side_effects=True, vmem_limit_bytes=65400 * 1024),
    )(
        windows.T,
        q_gain.reshape(1, share),
        k_gain.reshape(1, share),
        q_raw.reshape(flat),
        k_raw.reshape(flat),
        values.reshape(flat),
        d_out.reshape(flat),
    )
    fields = pl.pallas_call(
        store,
        out_shape=[field] * 4,
        in_specs=[pl.BlockSpec(memory_space=pl.ANY)] * 4,
        out_specs=[hbm] * 4,
        scratch_shapes=[dma((4,))],
    )(*fields)
    return tuple(one.reshape(q_raw.shape) for one in fields) + (q_part[0], k_part[0])


def solution(mesh):
    axes = tuple(mesh.shape[name] for name in ("fsdp", "ty", "tx"))
    spec = P("fsdp", "ty", "tx", None)
    return jax.shard_map(
        functools.partial(body, axes),
        mesh=mesh,
        in_specs=(spec, spec, spec, spec, P("fsdp"), P("fsdp"), P()),
        out_specs=(spec, spec, spec, spec, P("fsdp"), P("fsdp")),
        check_vma=False,
    )
```

```python
import functools
import math

import jax
import jax.numpy as jnp
from jax import lax
from jax.experimental import pallas as pl
from jax.experimental.pallas import tpu as pltpu
from jax.sharding import PartitionSpec as P

TILE = 8
NORM_EPS = 1e-06
CLOSED = -1e30
MESH = pl.DeviceIdType.MESH
V, K, D, Q = 0, 1, 2, 3
UNROLL = 3
HALVES = 2


def dot_nt(left, right):
    return lax.dot_general(
        left, right, (((1,), (1,)), ((), ())), preferred_element_type=jnp.float32
    )


def dot_nn(left, right):
    return lax.dot_general(
        left, right, (((1,), (0,)), ((), ())), preferred_element_type=jnp.float32
    )


def norm_parts(raw):
    floats = raw.astype(jnp.float32)
    inverse = lax.rsqrt(jnp.mean(floats * floats, axis=-1, keepdims=True) + NORM_EPS)
    return floats * inverse, inverse


def when(cond, act):
    if cond is None:
        act()
    else:
        pl.when(cond)(act)


def both(one, two):
    if one is None:
        return two
    if two is None:
        return one
    return jnp.logical_and(one, two)


def kernel(
    dims,
    win_ref,
    q_gain_ref,
    k_gain_ref,
    q_hbm,
    k_hbm,
    v_hbm,
    d_hbm,
    out_hbm,
    qg_hbm,
    kg_hbm,
    vg_hbm,
    q_part_ref,
    k_part_ref,
    near,
    stat,
    srow,
    bias,
    gains,
    q_ref,
    k_ref,
    out_ref,
    qg_ref,
    kg_ref,
    vg_ref,
    sums,
    load_sem,
    save_sem,
    gain_send,
    gain_recv,
    sum_send,
    sum_recv,
    x_send,
    x_recv,
    ty_send,
    ty_recv,
):
    fsdp, ty, tx, frames, rows, heads, size, slots = dims
    width = heads * size
    parts = frames * HALVES
    group = heads // HALVES
    wide = group * size
    z = lax.axis_index("fsdp")
    t = lax.axis_index("ty")
    x = lax.axis_index("tx")
    scale = 1.0 / math.sqrt(size)
    exp_scale = scale * math.log2(math.e)

    if tx == 1:
        x_links = []
    elif tx == 2:
        x_links = [(1, 1 - x, None, None)]
    else:
        x_links = [(1, x + 1, x < tx - 1, x > 0), (2, x - 1, x > 0, x < tx - 1)]
    ty_links = [(1, t + 1, t < ty - 1, t > 0), (2, t - 1, t > 0, t < ty - 1)]

    barrier = pltpu.get_barrier_semaphore()

    def greet(device):
        pl.semaphore_signal(barrier, inc=1, device_id=device, device_id_type=MESH)

    plane = [
        ({"ty": lax.rem(t + i, ty), "tx": lax.rem(x + j, tx)})
        for i in range(ty) for j in range(tx) if i or j
    ]
    line = [{"fsdp": lax.rem(z + i, fsdp)} for i in range(1, fsdp)]
    groups = ((plane, t * tx + x), (line, z))
    for peers, _ in groups:
        for peer in peers:
            greet(peer)

    loads = [
        pltpu.make_async_copy(source.at[frame * rows:(frame + 1) * rows], target, load_sem.at[i])
        for i, (source, frame, target) in enumerate(
            [(v_hbm, frame, near.at[V, frame, 0:rows]) for frame in range(frames)]
            + [(k_hbm, frame, k_ref.at[frame * rows:(frame + 1) * rows]) for frame in range(frames)]
            + [(d_hbm, frame, near.at[D, frame, 0:rows]) for frame in range(frames)]
            + [(q_hbm, frame, q_ref.at[frame * rows:(frame + 1) * rows]) for frame in range(frames)])
    ]
    for load in loads:
        load.start()

    def block(buffer, chunk, slot):
        if buffer is stat:
            return stat.at[chunk, slot]
        array, part = chunk
        frame, half = divmod(part, HALVES)
        return near.at[array, frame, pl.ds(slot * rows, rows), pl.ds(half * wide, wide)]

    def sem_index(buffer, chunk):
        if buffer is stat:
            return 4 * parts + chunk
        return chunk[0] * parts + chunk[1]

    def x_copy(link, buffer, chunk):
        column, peer, _, _ = link
        s = sem_index(buffer, chunk)
        return pltpu.make_async_remote_copy(
            src_ref=block(buffer, chunk, 0),
            dst_ref=block(buffer, chunk, 3 * column),
            send_sem=x_send.at[column - 1, s],
            recv_sem=x_recv.at[column - 1, s],
            device_id={"tx": peer},
            device_id_type=MESH,
        )

    def ty_copy(link, column, buffer, chunk):
        row, peer, _, _ = link
        s = sem_index(buffer, chunk)
        return pltpu.make_async_remote_copy(
            src_ref=block(buffer, chunk, 3 * column),
            dst_ref=block(buffer, chunk, 3 * column + row),
            send_sem=ty_send.at[row - 1, column, s],
            recv_sem=ty_recv.at[row - 1, column, s],
            device_id={"ty": peer},
            device_id_type=MESH,
        )

    def start_x(buffer, chunk):
        for link in x_links:
            when(link[2], lambda link=link: x_copy(link, buffer, chunk).start())

    def start_ty(buffer, chunk):
        for link in ty_links:
            when(link[2], lambda link=link: ty_copy(link, 0, buffer, chunk).start())

    def forward(buffer, chunk):
        for x_link in x_links:
            when(x_link[3], lambda x_link=x_link: x_copy(x_link, buffer, chunk).wait_recv())
            for link in ty_links:
                when(
                    both(link[2], x_link[3]),
                    lambda link=link, x_link=x_link: ty_copy(
                        link, x_link[0], buffer, chunk).start(),
                )

    def arrive(buffer, chunk):
        for link in ty_links:
            when(link[3], lambda link=link: ty_copy(link, 0, buffer, chunk).wait_recv())
            for x_link in x_links:
                when(
                    both(link[3], x_link[3]),
                    lambda link=link, x_link=x_link: ty_copy(
                        link, x_link[0], buffer, chunk).wait_recv(),
                )

    def finish(buffer, chunk):
        for link in x_links:
            when(link[2], lambda link=link: x_copy(link, buffer, chunk).wait_send())
        for link in ty_links:
            when(link[2], lambda link=link: ty_copy(link, 0, buffer, chunk).wait_send())
            for x_link in x_links:
                when(
                    both(link[2], x_link[3]),
                    lambda link=link, x_link=x_link: ty_copy(
                        link, x_link[0], buffer, chunk).wait_send(),
                )

    def clear(slot):
        near[:, :, slot * rows:(slot + 1) * rows, :] = jnp.zeros(
            (4, frames, rows, width), near.dtype)
        stat[:, slot] = jnp.zeros((parts,) + stat.shape[2:], stat.dtype)

    exists = [None] * slots
    for column in range(slots // 3):
        have_column = None
        for link in x_links:
            if link[0] == column:
                have_column = link[3]
        exists[3 * column] = have_column
        for link in ty_links:
            exists[3 * column + link[0]] = both(link[3], have_column)
    for slot in range(slots):
        if slot >= 3 * (slots // 3):
            exists[slot] = False
            clear(slot)
        elif exists[slot] is not None:
            pl.when(jnp.logical_not(exists[slot]))(functools.partial(clear, slot))

    lane = lax.broadcasted_iota(jnp.int32, (1, 2 * rows), 1)
    for head in range(heads):
        row_bias = jnp.where(win_ref[0, head] >= 3, 0.0, CLOSED)
        col_bias = jnp.where(win_ref[1, head] >= 3, 0.0, CLOSED)
        terms = []
        for slot in range(slots):
            term = jnp.float32(0.0)
            if slot % 3 != 0:
                term = term + row_bias
            if slot // 3 != 0:
                term = term + col_bias
            if exists[slot] is False:
                term = jnp.float32(CLOSED)
            elif exists[slot] is not None:
                term = term + jnp.where(exists[slot], 0.0, CLOSED)
            terms.append(term)
        for pair in range(slots // 2):
            bias[head:head + 1, pair * 2 * rows:(pair + 1) * 2 * rows] = jnp.where(
                lane < rows, terms[2 * pair], terms[2 * pair + 1])

    share = size // fsdp
    gains[z] = jnp.zeros((8, size), jnp.float32)
    gains[z, 0:1, 0:share] = q_gain_ref[...]
    gains[z, 1:2, 0:share] = k_gain_ref[...]
    gains[z] = pltpu.roll(gains[z], z * share, 1)

    pl.semaphore_wait(barrier, len(plane) + len(line))

    def gain_copy(step):
        return pltpu.make_async_remote_copy(
            src_ref=gains.at[z],
            dst_ref=gains.at[z],
            send_sem=gain_send.at[step - 1],
            recv_sem=gain_recv.at[step - 1],
            device_id={"fsdp": lax.rem(z + step, fsdp)},
            device_id_type=MESH,
        )

    for step in range(1, fsdp):
        gain_copy(step).start()
    for frame in range(frames):
        loads[frame].wait()
        for half in range(HALVES):
            start_x(near, (V, frame * HALVES + half))
            start_ty(near, (V, frame * HALVES + half))
    for load in loads[frames:]:
        load.wait()
    for step in range(1, fsdp):
        gain_copy(step).wait()
    gain_all = jnp.sum(gains[...], axis=0)
    q_gain = gain_all[0:1]
    k_gain = gain_all[1:2]

    def place(source, array, frame, gain):
        for head in range(heads):
            cols = slice(head * size, (head + 1) * size)
            normed, _ = norm_parts(source[frame * rows:(frame + 1) * rows, cols])
            near[array, frame, 0:rows, cols] = (normed * gain).astype(near.dtype)

    for frame in range(frames):
        place(k_ref, K, frame, k_gain)
        for half in range(HALVES):
            start_x(near, (K, frame * HALVES + half))
            start_ty(near, (K, frame * HALVES + half))
    for frame in range(frames):
        place(q_ref, Q, frame, q_gain)
        for half in range(HALVES):
            start_x(near, (D, frame * HALVES + half))
            start_x(near, (Q, frame * HALVES + half))

    def saves(pairs, part):
        frame, half = divmod(part, HALVES)
        spot = (pl.ds(frame * rows, rows), pl.ds(half * wide, wide))
        return [
            pltpu.make_async_copy(source.at[spot], target.at[spot], save_sem.at[i, part])
            for i, source, target in pairs
        ]

    query_saves = [(0, out_ref, out_hbm), (1, qg_ref, qg_hbm)]
    key_saves = [(2, kg_ref, kg_hbm), (3, vg_ref, vg_hbm)]

    stat_lane = lax.broadcasted_iota(jnp.int32, (rows, stat.shape[3]), 1)

    def backward(raw, upstream, gain):
        normed, inverse = norm_parts(raw)
        part = jnp.sum(upstream * normed, axis=0, keepdims=True)
        scaled = upstream * gain
        mean = jnp.mean(scaled * normed, axis=-1, keepdims=True)
        return inverse * (scaled - normed * mean), part

    def query_head(frame, head, mark, held, part):
        cols = pl.ds(pl.multiple_of(head * size, size), size)
        span = slice(frame * rows, (frame + 1) * rows)
        keys = near[K, frame, :, cols]
        vals = near[V, frame, :, cols]
        queries = near[Q, frame, 0:rows, cols]
        grads = near[D, frame, 0:rows, cols]
        weights = jnp.exp2(dot_nt(queries, keys) * exp_scale + bias[pl.ds(head, 1), :])
        inverse = 1.0 / jnp.sum(weights, axis=-1, keepdims=True)
        shares = weights * inverse
        output = dot_nn(shares.astype(jnp.bfloat16), vals).astype(jnp.bfloat16)
        out_ref[span, cols] = output
        delta = jnp.sum(
            grads.astype(jnp.float32) * output.astype(jnp.float32), axis=-1, keepdims=True)
        share_grad = dot_nt(grads, vals)
        score_grad = (shares * (share_grad - delta)).astype(jnp.bfloat16)
        raw_grad, more = backward(
            q_ref[span, cols], dot_nn(score_grad, keys) * scale, q_gain)
        qg_ref[span, cols] = raw_grad.astype(jnp.bfloat16)
        held = jnp.where(stat_lane == mark, inverse, held)
        held = jnp.where(stat_lane == 8 + mark, delta, held)
        return held, part + more

    def query_side(chunk, part):
        frame, half = divmod(chunk, HALVES)

        def some(step, carry):
            held, part = carry
            for k in range(UNROLL):
                mark = step * UNROLL + k
                held, part = query_head(frame, half * group + mark, mark, held, part)
            return held, part

        held, part = lax.fori_loop(
            0, group // UNROLL, some,
            (jnp.zeros((rows, stat.shape[3]), jnp.float32), part))
        turned = jnp.transpose(jnp.concatenate([held, held], axis=0))
        stat[chunk, 0] = turned[0:stat.shape[2]]
        return part

    def key_head(frame, head, mark, part):
        cols = pl.ds(pl.multiple_of(head * size, size), size)
        span = slice(frame * rows, (frame + 1) * rows)
        keys = near[K, frame, 0:rows, cols]
        vals = near[V, frame, 0:rows, cols]
        queries = near[Q, frame, :, cols]
        grads = near[D, frame, :, cols]
        weights = jnp.exp2(dot_nt(keys, queries) * exp_scale + bias[pl.ds(head, 1), :])
        shares = weights * srow[pl.ds(mark, 1), :]
        vg_ref[span, cols] = dot_nn(shares.astype(jnp.bfloat16), grads).astype(jnp.bfloat16)
        share_grad = dot_nt(vals, grads)
        score_grad = (shares * (share_grad - srow[pl.ds(8 + mark, 1), :])).astype(jnp.bfloat16)
        raw_grad, more = backward(
            k_ref[span, cols], dot_nn(score_grad, queries) * scale, k_gain)
        kg_ref[span, cols] = raw_grad.astype(jnp.bfloat16)
        return part + more

    def key_side(chunk, part):
        frame, half = divmod(chunk, HALVES)
        side = lax.broadcasted_iota(jnp.int32, (stat.shape[2], 2 * rows), 1)
        for pair in range(slots // 2):
            srow[:, pair * 2 * rows:(pair + 1) * 2 * rows] = jnp.where(
                side < rows, stat[chunk, 2 * pair], stat[chunk, 2 * pair + 1])

        def some(step, part):
            for k in range(UNROLL):
                mark = step * UNROLL + k
                part = key_head(frame, half * group + mark, mark, part)
            return part

        return lax.fori_loop(0, group // UNROLL, some, part)

    steps = [(V, K, chunk) for chunk in range(parts)]
    steps += [(D, Q, chunk) for chunk in range(parts)]

    def forward_step(first, second, chunk):
        forward(near, (first, chunk))
        forward(near, (second, chunk))
        if first == V:
            start_ty(near, (D, chunk))
            start_ty(near, (Q, chunk))
        else:
            forward(stat, chunk)

    q_part = jnp.zeros((1, size), jnp.float32)
    part = jnp.zeros((1, size), jnp.float32)
    forward_step(*steps[0])
    for place_in, (first, second, chunk) in enumerate(steps):
        if place_in + 1 < len(steps):
            forward_step(*steps[place_in + 1])
        arrive(near, (first, chunk))
        arrive(near, (second, chunk))
        if first == V:
            q_part = query_side(chunk, q_part)
            start_x(stat, chunk)
            start_ty(stat, chunk)
            for save in saves(query_saves, chunk):
                save.start()
        else:
            arrive(stat, chunk)
            part = key_side(chunk, part)
            for save in saves(key_saves, chunk):
                save.start()
    side = lax.broadcasted_iota(jnp.int32, (8, size), 0)
    total = jnp.where(side == 0, q_part, jnp.where(side == 1, part, 0.0))
    first = 0
    for peers, place_in in groups:
        count = len(peers) + 1
        if count > 1:
            sums[first + place_in] = total

            def sum_copy(step, peers=peers, place_in=place_in, first=first):
                return pltpu.make_async_remote_copy(
                    src_ref=sums.at[first + place_in],
                    dst_ref=sums.at[first + place_in],
                    send_sem=sum_send.at[first + step],
                    recv_sem=sum_recv.at[first + step],
                    device_id=peers[step - 1],
                    device_id_type=MESH,
                )

            for step in range(1, count):
                sum_copy(step).start()
            for step in range(1, count):
                sum_copy(step).wait()
            total = jnp.sum(sums[first:first + count], axis=0)
        first += count
    owned = pltpu.roll(total, lax.rem(size - z * share, size), 1)
    q_part_ref[...] = owned[0:1, 0:share]
    k_part_ref[...] = owned[1:2, 0:share]

    for chunk in range(parts):
        for array in range(4):
            finish(near, (array, chunk))
        finish(stat, chunk)
        for save in saves(query_saves + key_saves, chunk):
            save.wait()


def store(*refs):
    count = len(refs) // 2
    for i in range(count):
        refs[count + i][...] = refs[i][...]


def body(axes, q_raw, k_raw, values, d_out, q_gain, k_gain, windows):
    fsdp, ty, tx = axes
    frames, height, across, width = q_raw.shape
    rows = height * across
    heads = windows.shape[0]
    size = width // heads
    columns = min(tx, 3)
    slots = 3 * columns + (3 * columns) % 2
    share = q_gain.shape[0]
    flat = (frames * rows, width)
    field = jax.ShapeDtypeStruct(flat, jnp.bfloat16)
    vmem = pl.BlockSpec(memory_space=pltpu.VMEM)
    sems = 5 * frames * HALVES
    dims = (fsdp, ty, tx, frames, rows, heads, size, slots)
    dma = pltpu.SemaphoreType.DMA
    side = max(columns - 1, 1)
    hbm = pl.BlockSpec(memory_space=pltpu.HBM)
    gain_field = jax.ShapeDtypeStruct((1, share), jnp.float32)
    peers = fsdp + ty * tx
    results = pl.pallas_call(
        functools.partial(kernel, dims),
        out_shape=[field] * 4 + [gain_field] * 2,
        in_specs=[pl.BlockSpec(memory_space=pltpu.SMEM)] + [vmem] * 2 + [hbm] * 4,
        out_specs=[hbm] * 4 + [vmem] * 2,
        scratch_shapes=[
            pltpu.VMEM((4, frames, slots * rows, width), jnp.bfloat16),
            pltpu.VMEM((frames * HALVES, slots, 16, 2 * rows), jnp.float32),
            pltpu.VMEM((16, slots * rows), jnp.float32),
            pltpu.VMEM((16, slots * rows), jnp.float32),
            pltpu.VMEM((fsdp, 8, size), jnp.float32),
            *[pltpu.VMEM(flat, jnp.bfloat16) for _ in range(6)],
            pltpu.VMEM((peers, 8, size), jnp.float32),
            dma((4 * frames,)),
            dma((4, frames * HALVES)),
            dma((max(fsdp - 1, 1),)),
            dma((max(fsdp - 1, 1),)),
            dma((peers,)),
            dma((peers,)),
            dma((side, sems)),
            dma((side, sems)),
            dma((2, columns, sems)),
            dma((2, columns, sems)),
        ],
        compiler_params=pltpu.CompilerParams(
            collective_id=0, has_side_effects=True, vmem_limit_bytes=65400 * 1024),
    )(
        windows.T,
        q_gain.reshape(1, share),
        k_gain.reshape(1, share),
        q_raw.reshape(flat),
        k_raw.reshape(flat),
        values.reshape(flat),
        d_out.reshape(flat),
    )
    tall = frames * rows // 2
    blocks = [pl.BlockSpec((tall, width), lambda i: (i, 0))] * 4
    blocks += [pl.BlockSpec((1, share), lambda i: (0, 0))] * 2
    *fields, q_part, k_part = pl.pallas_call(
        store,
        out_shape=[field] * 4 + [gain_field] * 2,
        grid=(2,),
        in_specs=blocks,
        out_specs=blocks,
    )(*results)
    return tuple(one.reshape(q_raw.shape) for one in fields) + (q_part[0], k_part[0])


def solution(mesh):
    axes = tuple(mesh.shape[name] for name in ("fsdp", "ty", "tx"))
    spec = P("fsdp", "ty", "tx", None)
    return jax.shard_map(
        functools.partial(body, axes),
        mesh=mesh,
        in_specs=(spec, spec, spec, spec, P("fsdp"), P("fsdp"), P()),
        out_specs=(spec, spec, spec, spec, P("fsdp"), P("fsdp")),
        check_vma=False,
    )
```
